32 devices in a mesh: src: 16 (over z, y, x), fac: 2 (over core).
Axes of the slice: x: 2, y: 2, z: 4, core: 2. Of those that a mesh axis runs over, the one named last changes fastest.
Arguments:
- lower_inverse: bfloat16 [2, 1024, 2, 1024], P('fac', 'src'), as said below
- coupling: bfloat16 [2, 1024, 2, 1024], P('fac', 'src'), as said below
- source_cell: int32 [2048], P('src'), may hold values from 0 to 2047
- source_wave: float32 [2048, 2], P('src'), may hold values from -6 to 6
- inflow_field: bfloat16 [2048, 2, 1024], P('src'), may hold values from -6 to 6
- receiver_cell: int32 [2048, 128], P('src'), may hold values from 0 to 2047
- observed: float32 [2048, 2, 128], P('src'), may hold values from -6 to 6
- adjoint: bfloat16 [2048, 2, 2, 1024], P('src', 'fac'), may hold values from -6 to 6
Outputs:
- wavefield: float32 [2048, 2, 2, 1024], P('src', 'fac')
- data_residual: float32 [2048, 2, 128], P('src')
- gradient: float32 [2, 1024], P('fac', 'src')
The draws below stay inside these ranges and needn't reach their ends.
Inputs may be any that keep to these rules, and one draw needn't show every extreme that they name: lower_inverse[i, j, p, k] is zero where k > j. coupling[i, j, p, k] is zero where k < j.
All inputs are finite; a program needn't handle non-finite values.
Results may differ from the reference program's by a relative error of at most 0.025.
Values may be sent and summed in bfloat16 or wider, within the bound.
A program may use at most 64 MiB of HBM per device.

```python
import math
import jax
import jax.numpy as jnp
from jax import lax

BW = 1024
NREC = 128
NB = 2
NS = 2048


def draw_lower_inverse(key, part):
    first, second, third = jax.random.split(jax.random.fold_in(key, 11), 3)
    row_ids = jnp.arange(BW)[:, None]
    col_ids = jnp.arange(BW)[None, :]
    offdiag = jax.random.normal(first, (NB, 2, BW, BW), jnp.float32)
    real_diag = jax.random.uniform(second, (NB, BW), jnp.float32, 0.8, 1.25)
    imag_diag = jax.random.uniform(third, (NB, BW), jnp.float32, -0.3, 0.3)
    offdiag = offdiag * (0.5 / math.sqrt(BW))
    diagonal = jnp.stack([real_diag, imag_diag], axis=1)
    result = jnp.where(row_ids > col_ids, offdiag, 0.0) + jnp.where(row_ids == col_ids, diagonal[:, :, :, None], 0.0)
    return jnp.transpose(result, (0, 2, 1, 3)).astype(jnp.bfloat16)


def draw_coupling(key, part):
    first = jax.random.fold_in(key, 23)
    row_ids = jnp.arange(BW)[:, None]
    col_ids = jnp.arange(BW)[None, :]
    entries = jax.random.normal(first, (NB, 2, BW, BW), jnp.float32)
    entries = entries * (1.0 / math.sqrt(BW))
    result = jnp.where(row_ids <= col_ids, entries, 0.0)
    return jnp.transpose(result, (0, 2, 1, 3)).astype(jnp.bfloat16)


def place_ends(values, stream_key, low, largest):
    place = [jax.random.randint(jax.random.fold_in(stream_key, axis), (), 0, length) for axis, length in enumerate(values.shape)]
    main_axis = values.shape.index(max(values.shape))
    beside = place[:main_axis] + [(place[main_axis] + 1) % values.shape[main_axis]] + place[main_axis + 1:]
    return values.at[tuple(place)].set(low).at[tuple(beside)].set(largest)


def strengthened(values, stream_key, source, target, parts, factor):
    owner, partner = [(jnp.arange(values.shape[position]) // (values.shape[position] // parts)).reshape([-1 if axis == position else 1 for axis in range(values.ndim)]) for position in (source, target)]
    chosen = jax.random.permutation(stream_key, parts)[partner]
    strong = (owner == chosen) | (owner == (partner + parts // 2) % parts)
    return jnp.where(strong, factor * values, values)


def level_of(rng, shape, cuts, low, high):
    level, own = 1.0, jax.random.fold_in(rng, 6)
    for axis_at, shards_of in cuts:
        draws = jnp.exp(jax.random.uniform(jax.random.fold_in(own, axis_at), (shards_of,), jnp.float32, low / len(cuts), high / len(cuts)))
        level = level * jnp.repeat(draws, shape[axis_at] // shards_of).reshape([-1 if axis == axis_at else 1 for axis in range(len(shape))])
    return level


def bell_draw(key, extent, deviation, bound, shards=(), kind=jnp.bfloat16):
    values = deviation * jax.random.normal(key, extent, jnp.float32)
    if shards:
        values = values * level_of(key, extent, shards, -0.22, 0.18)
    return jnp.clip(values, -bound, bound).astype(kind)


def noise_with(stream_key, dims, scale, reach, cuts, heavy, kind=jnp.bfloat16):
    values = scale * jax.random.normal(stream_key, dims, jnp.float32)
    if cuts:
        values = values * level_of(stream_key, dims, cuts, -0.22, 0.18)
    return jnp.clip(strengthened(values, jax.random.fold_in(stream_key, 3), *heavy), -reach, reach).astype(kind)


def setup_inputs(seed: int = 0) -> dict:
    keys = jax.random.split(jax.random.key(seed), 9)
    lower_inverse = draw_lower_inverse(jax.random.fold_in(keys[8], 71), 0)
    coupling = draw_coupling(jax.random.fold_in(keys[8], 71), 0)
    source_cell = place_ends(jax.random.randint(keys[2], (NS,), 0, NB * BW), jax.random.fold_in(keys[2], 1), 0, (NB * BW) - 1).astype(jnp.int32)
    source_wave = bell_draw(keys[3], (NS, 2), 1.0, 6.0, ((0, 16),), jnp.float32)
    inflow_field = bell_draw(keys[4], (NS, 2, BW), 1.0, 6.0, ((0, 16),))
    receiver_cell = place_ends(jax.random.randint(keys[5], (NS, NREC), 0, NB * BW), jax.random.fold_in(keys[5], 1), 0, (NB * BW) - 1).astype(jnp.int32)
    observed = bell_draw(keys[6], (NS, 2, NREC), 1.0, 6.0, ((0, 16),), jnp.float32)
    adjoint = noise_with(keys[7], (NS, NB, 2, BW), 1.0, 6.0, ((0, 16), (1, 2)), (0, 3, 16, 2.0))
    return {"lower_inverse": lower_inverse, "coupling": coupling, "source_cell": source_cell, "source_wave": source_wave, "inflow_field": inflow_field, "receiver_cell": receiver_cell, "observed": observed, "adjoint": adjoint}


def complex_apply(vector, matrix):
    width = matrix.shape[0]
    joined = matrix.reshape(width, 2 * width)
    real_row = jnp.concatenate([vector[:, 0], -vector[:, 1]], axis=1)
    imag_row = jnp.concatenate([vector[:, 1], vector[:, 0]], axis=1)
    stacked = jnp.stack([real_row, imag_row], axis=1).reshape(-1, 2 * width)
    contract_dims = (((1,), (1,)), ((), ()))
    result = lax.dot_general(stacked, joined, contract_dims, preferred_element_type=jnp.float32)
    return result.reshape(vector.shape[0], 2, width)

def reference(lower_inverse, coupling, source_cell, source_wave, inflow_field, receiver_cell, observed, adjoint):
    previous = inflow_field
    blocks = []
    slabs = []
    picked = jnp.zeros(observed.shape, jnp.float32)
    scale = 1.0 / math.sqrt(NS)
    for block in range(NB):
        cell_ids = block * BW + jnp.arange(BW, dtype=jnp.int32)
        hit = source_cell[:, None] == cell_ids[None, :]
        source_term = jnp.where(hit[:, None, :], source_wave[:, :, None], jnp.zeros((), jnp.float32))
        reduced = (source_term - complex_apply(previous, coupling[block])).astype(jnp.bfloat16)
        field = complex_apply(reduced, lower_inverse[block])
        blocks.append(field)
        previous = field.astype(jnp.bfloat16)
        local_ids = receiver_cell - block * BW
        inside = (local_ids >= 0) & (local_ids < BW)
        clipped = jnp.clip(local_ids, 0, BW - 1).astype(jnp.int32)
        index_both = jnp.broadcast_to(clipped[:, None, :], observed.shape)
        values = jnp.take_along_axis(field, index_both, axis=2)
        picked = picked + jnp.where(inside[:, None, :], values, jnp.zeros((), jnp.float32))
        slabs.append(lax.optimization_barrier(jnp.sum(field * adjoint[:, block].astype(jnp.float32), axis=(0, 1))) * scale)
    wavefield = jnp.stack(blocks, axis=1)
    return (wavefield, picked - observed, jnp.stack(slabs, axis=0))
```

```python
import functools
import math

import jax
import jax.numpy as jnp
from jax import lax
from jax.experimental import pallas as pl
from jax.experimental.pallas import tpu as pltpu
from jax.sharding import PartitionSpec as P

MESH = pl.DeviceIdType.MESH
LANES = 128
UP, DOWN, ACROSS_X, ACROSS_Y = range(4)
PLANE, LAYERS = 4, 4


def from_behind(shard, axis, by):
    size = lax.axis_size(axis)
    pairs = [(i, i + by) for i in range(size) if 0 <= i + by < size]
    return lax.ppermute(shard, axis, pairs)


def complex_apply(vector, matrix):
    width = matrix.shape[0]
    joined = matrix.reshape(width, 2 * width)
    real_row = jnp.concatenate([vector[:, 0], -vector[:, 1]], axis=1)
    imag_row = jnp.concatenate([vector[:, 1], vector[:, 0]], axis=1)
    stacked = jnp.stack([real_row, imag_row], axis=1).reshape(-1, 2 * width)
    contract_dims = (((1,), (1,)), ((), ()))
    result = lax.dot_general(stacked, joined, contract_dims, preferred_element_type=jnp.float32)
    return result.reshape(vector.shape[0], 2, width)


def source_block(cells, wave, owner, width):
    cell_ids = owner * width + lax.broadcasted_iota(jnp.int32, (width,), 0)
    hit = cells[:, None] == cell_ids[None, :]
    return jnp.where(hit[:, None, :], wave[:, :, None], jnp.zeros((), jnp.float32))


def block_solve(previous, cells, wave, owner, lower_full, coupling_full):
    width = lower_full.shape[0]
    term = source_block(cells, wave, owner, width)
    reduced = (term - complex_apply(previous, coupling_full)).astype(jnp.bfloat16)
    return complex_apply(reduced, lower_full)


def plain_device(
    lower_inverse,
    coupling,
    source_cell,
    source_wave,
    inflow_field,
    receiver_cell,
    observed,
    adjoint,
):
    owner = lax.axis_index("fac")
    fac_count = lax.axis_size("fac")
    width = lower_inverse.shape[3]
    sources = source_cell.shape[0]
    whole_lower, whole_coupling = (
        lax.all_gather(lower_inverse, "src", axis=1, tiled=True),
        lax.all_gather(coupling, "src", axis=1, tiled=True),
    )
    lower_full = whole_lower[0]
    coupling_full = whole_coupling[0]
    empty_field = jnp.zeros((sources, 2, width), jnp.float32)

    def section_step(section, carry):
        current, received = carry

        def compute():
            return block_solve(received, source_cell, source_wave, owner, lower_full, coupling_full)

        def unchanged():
            return current

        current = lax.cond(section == owner, compute, unchanged)
        received = from_behind(current.astype(jnp.bfloat16), "fac", 1)
        return (current, received)

    current, received = lax.fori_loop(0, fac_count, section_step, (empty_field, inflow_field))
    local_ids = receiver_cell - owner * width
    inside = (local_ids >= 0) & (local_ids < width)
    clipped = jnp.clip(local_ids, 0, width - 1)
    index_both = jnp.broadcast_to(clipped[:, None, :], observed.shape)
    values = jnp.take_along_axis(current, index_both, axis=2)
    values = jnp.where(inside[:, None, :], values, jnp.zeros((), jnp.float32))
    picked = lax.psum(values.astype(jnp.bfloat16), "fac").astype(jnp.float32)
    scale = 1.0 / math.sqrt(sources * lax.axis_size("src"))
    terms = jnp.sum(current * adjoint[:, 0].astype(jnp.float32), axis=(0, 1)) * scale
    gradient = lax.psum_scatter(terms[None, :], "src", scatter_dimension=1, tiled=True)
    return (current[:, None], picked - observed, gradient)


def window_kernel(
    scale, packed, diagonal, inflow, cell, wave, receivers, observed, adjoint,
    field, residual, slab,
    rows_all, diag_all, diag_rows, incoming, reduced, outgoing, terms, terms_all, picked, picked_other,
    row_send, row_recv, diag_send, diag_recv, term_send, term_recv, pair_send, pair_recv,
):
    me, owner = lax.axis_index("src"), lax.axis_index("fac")
    shards = PLANE * LAYERS
    x, y, z = me % 2, (me // 2) % 2, me // PLANE
    x_step, y_step = 1 - 2 * x, 2 - 4 * y
    _, sources, width = field.shape
    rows = packed.shape[1]
    per = LANES // rows
    tile = min(256, width)

    barrier = pltpu.get_barrier_semaphore()

    @pl.loop(1, shards)
    def _(offset):
        pl.semaphore_signal(barrier, inc=1, device_id=((me + offset) % shards, owner), device_id_type=MESH)

    pl.semaphore_signal(barrier, inc=1, device_id=(me, 1 - owner), device_id_type=MESH)
    pl.semaphore_wait(barrier, shards)

    def row_copy(way, slot, half, target, own=False):
        return pltpu.make_async_remote_copy(
            src_ref=packed.at[half] if own else rows_all.at[slot, half],
            dst_ref=rows_all.at[slot, half],
            send_sem=row_send.at[way, slot, half],
            recv_sem=row_recv.at[slot, half],
            device_id=(target, owner),
            device_id_type=MESH,
        )

    def arrived(slot, half):
        row_copy(ACROSS_X, slot, half, me + x_step).wait_recv()

    def along_z(way, slot, act, own=False):
        step = PLANE if way == UP else -PLANE

        @pl.when(z < LAYERS - 1 if way == UP else z > 0)
        def _():
            for half in range(2):
                act(row_copy(way, slot, half, me + step, own))

    def in_plane(slot, act, own=False):
        act(row_copy(ACROSS_X, slot, 0, me + x_step, own))
        act(row_copy(ACROSS_Y, slot, 1, me + y_step, own))
        act(row_copy(ACROSS_Y, slot, 0, me + y_step, own))
        act(row_copy(ACROSS_X, slot, 1, me + x_step, own))

    def relay(slot_x, slot_y, act, wait):
        if wait:
            arrived(slot_x, 0)
        act(row_copy(ACROSS_Y, slot_x, 0, me + y_step))
        if wait:
            arrived(slot_y, 1)
        act(row_copy(ACROSS_X, slot_y, 1, me + x_step))

    def layers_at(step, visit):
        if step == 0:
            visit(me, None)
            return

        @pl.when(z >= step)
        def _():
            visit(me - PLANE * step, UP)

        @pl.when(z + step < LAYERS)
        def _():
            visit(me + PLANE * step, DOWN)

    def gather_rows(act, wait):
        def first(slot, way):
            if way is None:
                along_z(UP, slot, act, True)
                along_z(DOWN, slot, act, True)
                in_plane(slot, act, True)
                return
            if wait:
                arrived(slot, 0)
                arrived(slot, 1)
            along_z(way, slot, act)
            in_plane(slot, act)

        def second(slot, way):
            relay(slot + x_step, slot + y_step, act, wait)

        layers_at(0, first)
        for step in range(1, LAYERS):
            layers_at(step, first)
            layers_at(step - 1, second)
        layers_at(LAYERS - 1, second)

    def diag_copy(offset, sender, target):
        return pltpu.make_async_remote_copy(
            src_ref=diagonal, dst_ref=diag_all.at[sender],
            send_sem=diag_send.at[offset], recv_sem=diag_recv.at[sender],
            device_id=(target, owner), device_id_type=MESH,
        )

    def term_copy(offset, sender, target):
        return pltpu.make_async_remote_copy(
            src_ref=terms.at[target // per], dst_ref=terms_all.at[sender],
            send_sem=term_send.at[offset], recv_sem=term_recv.at[sender],
            device_id=(target, owner), device_id_type=MESH,
        )

    def pair_copy(which, source, target):
        return pltpu.make_async_remote_copy(
            src_ref=source, dst_ref=target,
            send_sem=pair_send.at[which], recv_sem=pair_recv.at[which],
            device_id=(me, 1 - owner), device_id_type=MESH,
        )

    def to_all(make):
        @pl.loop(1, shards)
        def _(offset):
            make(offset, me, (me + offset) % shards).start()

    def wait_all(make):
        @pl.loop(1, shards)
        def _(offset):
            other = (me + offset) % shards
            make(offset, other, other).wait_recv()
            make(offset, me, other).wait_send()

    to_all(diag_copy)
    rows_all[me] = packed[...]
    diag_all[me] = diagonal[...]
    gather_rows(lambda copy: copy.start(), True)
    wait_all(diag_copy)
    for block in range(width // LANES):
        total = diag_all[block * per].astype(jnp.float32)
        for other in range(1, per):
            total += diag_all[block * per + other].astype(jnp.float32)
        diag_rows[:, block * LANES:(block + 1) * LANES] = total

    for layer in range(LAYERS):
        slot = me % PLANE + layer * PLANE
        arrived(slot + x_step, 1)
        arrived(slot + y_step, 0)
        arrived(slot + x_step + y_step, 0)
        arrived(slot + x_step + y_step, 1)

    handover = pair_copy(0, outgoing, incoming)

    @pl.when(owner == 0)
    def _():
        incoming[...] = inflow[...]

    @pl.when(owner > 0)
    def _():
        handover.wait_recv()

    contract = (((1,), (1,)), ((), ()))

    def matrix_tile(step, half):
        group = rows_all[pl.ds(step * (tile // rows), tile // rows), half]
        return group.reshape(tile, width)

    def masks(step):
        row = lax.broadcasted_iota(jnp.int32, (tile, width), 0) + step * tile
        return lax.broadcasted_iota(jnp.int32, (tile, width), 1), row

    def product(vector, first, second):
        with_first = lax.dot_general(vector, first, contract, preferred_element_type=jnp.float32)
        with_second = lax.dot_general(vector, second, contract, preferred_element_type=jnp.float32)
        return (
            with_first[:sources] - with_second[sources:],
            with_second[:sources] + with_first[sources:],
        )

    zero = jnp.zeros((), jnp.bfloat16)

    @pl.loop(0, width // tile)
    def _(step):
        column, row = masks(step)
        keep = column >= row
        parts = product(
            incoming[...].reshape(2 * sources, width),
            jnp.where(keep, matrix_tile(step, 0), zero),
            jnp.where(keep, matrix_tile(step, 1), zero),
        )
        at = pl.ds(pl.multiple_of(step * tile, tile), tile)
        ids = lax.broadcasted_iota(jnp.int32, (sources, tile), 1) + (owner * width + step * tile)
        hit = ids == cell[...]
        for part in range(2):
            term = jnp.where(hit, wave[part], 0.0)
            reduced[part, :, at] = (term - parts[part]).astype(jnp.bfloat16)

    @pl.loop(0, width // tile)
    def _(step):
        column, row = masks(step)
        keep = column < row
        real, imag = product(
            reduced[...].reshape(2 * sources, width),
            jnp.where(keep, matrix_tile(step, 0), zero),
            jnp.where(keep, matrix_tile(step, 1), zero),
        )
        at = pl.ds(pl.multiple_of(step * tile, tile), tile)
        red_real, red_imag = (reduced[part, :, at].astype(jnp.float32) for part in range(2))
        diag_real, diag_imag = diag_rows[0:1, at], diag_rows[1:2, at]
        real = real + (red_real * diag_real - red_imag * diag_imag)
        imag = imag + (red_real * diag_imag + red_imag * diag_real)
        field[0, :, at] = real
        field[1, :, at] = imag
        outgoing[0, :, at] = real.astype(jnp.bfloat16)
        outgoing[1, :, at] = imag.astype(jnp.bfloat16)
        total = real * adjoint[0, :, at].astype(jnp.float32) + imag * adjoint[1, :, at].astype(jnp.float32)
        total = jnp.sum(total.reshape(sources // 8, 8, tile), axis=0) * scale
        for block in range(tile // LANES):
            terms[step * (tile // LANES) + block] = total[:, block * LANES:(block + 1) * LANES]

    @pl.when(owner == 0)
    def _():
        handover.start()

    to_all(term_copy)
    local = receivers[...] - owner * width
    lane = local & (LANES - 1)
    home = local >> (LANES.bit_length() - 1)
    for part in range(2):
        values = jnp.zeros((sources, LANES), jnp.float32)
        for block in range(width // LANES):
            piece = field[part, :, block * LANES:(block + 1) * LANES]
            taken = jnp.take_along_axis(piece, lane, axis=1, mode="promise_in_bounds")
            values = jnp.where(home == block, taken, values)
        picked[part] = values.astype(jnp.bfloat16)
    swap = pair_copy(1, picked, picked_other)
    swap.start()

    wait_all(term_copy)
    total = terms[me // per]
    for offset in range(1, shards):
        total += terms_all[(me + offset) % shards]
    slab[...] = total

    gather_rows(lambda copy: copy.wait_send(), False)

    @pl.when(owner == 0)
    def _():
        handover.wait_send()

    swap.wait()
    both = picked[...].astype(jnp.float32) + picked_other[...].astype(jnp.float32)
    residual[...] = both - observed[...]


def per_device(
    lower_inverse,
    coupling,
    source_cell,
    source_wave,
    inflow_field,
    receiver_cell,
    observed,
    adjoint,
):
    me = lax.axis_index("src")
    shards = lax.axis_size("src")
    _, rows, _, width = lower_inverse.shape
    sources, receivers = receiver_cell.shape
    row_ids = me * rows + lax.broadcasted_iota(jnp.int32, (rows, width), 0)
    col_ids = lax.broadcasted_iota(jnp.int32, (rows, width), 1)
    lower = jnp.transpose(lower_inverse[0], (1, 0, 2))
    packed = jnp.where(col_ids < row_ids, lower, jnp.transpose(coupling[0], (1, 0, 2)))
    square = lax.dynamic_slice_in_dim(lower_inverse[0], me * rows, rows, axis=2)
    line = jnp.arange(rows)
    own = jnp.where((line[:, None] == line[None, :])[:, None, :], square, jnp.zeros((), square.dtype))
    own = jnp.sum(own.astype(jnp.float32), axis=0).astype(jnp.bfloat16)
    per = LANES // rows
    diagonal = lax.dynamic_update_slice(
        jnp.zeros((16, LANES), jnp.bfloat16), own, (jnp.int32(0), (me % per) * rows)
    )
    both = (2, sources, width)
    dma = pltpu.SemaphoreType.DMA
    vmem = pl.BlockSpec(memory_space=pltpu.VMEM)
    scale = 1.0 / math.sqrt(sources * shards)
    field, residual, slab = pl.pallas_call(
        functools.partial(window_kernel, scale),
        out_shape=(
            jax.ShapeDtypeStruct(both, jnp.float32),
            jax.ShapeDtypeStruct((2, sources, receivers), jnp.float32),
            jax.ShapeDtypeStruct((8, LANES), jnp.float32),
        ),
        in_specs=[vmem] * 8,
        out_specs=(vmem,) * 3,
        scratch_shapes=[
            pltpu.VMEM((shards, 2, rows, width), jnp.bfloat16),
            pltpu.VMEM((shards, 16, LANES), jnp.bfloat16),
            pltpu.VMEM((16, width), jnp.float32),
            pltpu.VMEM(both, jnp.bfloat16),
            pltpu.VMEM(both, jnp.bfloat16),
            pltpu.VMEM(both, jnp.bfloat16),
            pltpu.VMEM((width // LANES, 8, LANES), jnp.float32),
            pltpu.VMEM((shards, 8, LANES), jnp.float32),
            pltpu.VMEM((2, sources, LANES), jnp.bfloat16),
            pltpu.VMEM((2, sources, LANES), jnp.bfloat16),
            dma((4, shards, 2)),
            dma((shards, 2)),
            dma((shards,)),
            dma((shards,)),
            dma((shards,)),
            dma((shards,)),
            dma((2,)),
            dma((2,)),
        ],
        compiler_params=pltpu.CompilerParams(
            collective_id=0, has_side_effects=True, vmem_limit_bytes=48 * 1024 * 1024
        ),
    )(
        packed,
        diagonal,
        jnp.transpose(inflow_field, (1, 0, 2)),
        source_cell[:, None],
        jnp.transpose(source_wave)[:, :, None],
        receiver_cell,
        jnp.transpose(observed, (1, 0, 2)),
        jnp.transpose(adjoint[:, 0], (1, 0, 2)),
    )
    gradient = lax.dynamic_slice_in_dim(jnp.sum(slab, axis=0), (me % per) * rows, rows)
    return (
        jnp.transpose(field, (1, 0, 2))[:, None],
        jnp.transpose(residual, (1, 0, 2)),
        gradient[None],
    )


def solution(mesh):
    fits = mesh.shape["src"] == PLANE * LAYERS and mesh.shape["fac"] == 2
    placed = (
        P("fac", "src", None, None),
        P("fac", "src", None, None),
        P("src"),
        P("src", None),
        P("src", None, None),
        P("src", None),
        P("src", None, None),
        P("src", "fac", None, None),
    )
    return jax.shard_map(
        per_device if fits else plain_device,
        mesh=mesh,
        in_specs=placed,
        out_specs=(P("src", "fac", None, None), P("src", None, None), P("fac", "src")),
        check_vma=False,
    )
```

```python
import functools
import math

import jax
import jax.numpy as jnp
from jax import lax
from jax.experimental import pallas as pl
from jax.experimental.pallas import tpu as pltpu
from jax.sharding import PartitionSpec as P

MESH = pl.DeviceIdType.MESH
LANES = 128
UP, DOWN, ACROSS_X, ACROSS_Y = range(4)
PLANE, LAYERS = 4, 4


def from_behind(shard, axis, by):
    size = lax.axis_size(axis)
    pairs = [(i, i + by) for i in range(size) if 0 <= i + by < size]
    return lax.ppermute(shard, axis, pairs)


def complex_apply(vector, matrix):
    width = matrix.shape[0]
    joined = matrix.reshape(width, 2 * width)
    real_row = jnp.concatenate([vector[:, 0], -vector[:, 1]], axis=1)
    imag_row = jnp.concatenate([vector[:, 1], vector[:, 0]], axis=1)
    stacked = jnp.stack([real_row, imag_row], axis=1).reshape(-1, 2 * width)
    contract_dims = (((1,), (1,)), ((), ()))
    result = lax.dot_general(stacked, joined, contract_dims, preferred_element_type=jnp.float32)
    return result.reshape(vector.shape[0], 2, width)


def source_block(cells, wave, owner, width):
    cell_ids = owner * width + lax.broadcasted_iota(jnp.int32, (width,), 0)
    hit = cells[:, None] == cell_ids[None, :]
    return jnp.where(hit[:, None, :], wave[:, :, None], jnp.zeros((), jnp.float32))


def block_solve(previous, cells, wave, owner, lower_full, coupling_full):
    width = lower_full.shape[0]
    term = source_block(cells, wave, owner, width)
    reduced = (term - complex_apply(previous, coupling_full)).astype(jnp.bfloat16)
    return complex_apply(reduced, lower_full)


def plain_device(
    lower_inverse,
    coupling,
    source_cell,
    source_wave,
    inflow_field,
    receiver_cell,
    observed,
    adjoint,
):
    owner = lax.axis_index("fac")
    fac_count = lax.axis_size("fac")
    width = lower_inverse.shape[3]
    sources = source_cell.shape[0]
    whole_lower, whole_coupling = (
        lax.all_gather(lower_inverse, "src", axis=1, tiled=True),
        lax.all_gather(coupling, "src", axis=1, tiled=True),
    )
    lower_full = whole_lower[0]
    coupling_full = whole_coupling[0]
    empty_field = jnp.zeros((sources, 2, width), jnp.float32)

    def section_step(section, carry):
        current, received = carry

        def compute():
            return block_solve(received, source_cell, source_wave, owner, lower_full, coupling_full)

        def unchanged():
            return current

        current = lax.cond(section == owner, compute, unchanged)
        received = from_behind(current.astype(jnp.bfloat16), "fac", 1)
        return (current, received)

    current, received = lax.fori_loop(0, fac_count, section_step, (empty_field, inflow_field))
    local_ids = receiver_cell - owner * width
    inside = (local_ids >= 0) & (local_ids < width)
    clipped = jnp.clip(local_ids, 0, width - 1)
    index_both = jnp.broadcast_to(clipped[:, None, :], observed.shape)
    values = jnp.take_along_axis(current, index_both, axis=2)
    values = jnp.where(inside[:, None, :], values, jnp.zeros((), jnp.float32))
    picked = lax.psum(values.astype(jnp.bfloat16), "fac").astype(jnp.float32)
    scale = 1.0 / math.sqrt(sources * lax.axis_size("src"))
    terms = jnp.sum(current * adjoint[:, 0].astype(jnp.float32), axis=(0, 1)) * scale
    gradient = lax.psum_scatter(terms[None, :], "src", scatter_dimension=1, tiled=True)
    return (current[:, None], picked - observed, gradient)


def window_kernel(
    scale, packed, diagonal, inflow, cell, wave, receivers, observed, adjoint,
    field, residual, slab,
    rows_all, diag_all, diag_rows, incoming, reduced, outgoing, terms, terms_all, picked, picked_other,
    row_send, row_recv, diag_send, diag_recv, term_send, term_recv, pair_send, pair_recv, turn,
):
    me, owner = lax.axis_index("src"), lax.axis_index("fac")
    shards = PLANE * LAYERS
    x, y, z = me % 2, (me // 2) % 2, me // PLANE
    x_step, y_step = 1 - 2 * x, 2 - 4 * y
    _, sources, width = field.shape
    rows = packed.shape[1]
    per = LANES // rows
    tile = PLANE * rows

    barrier = pltpu.get_barrier_semaphore()

    @pl.loop(1, shards)
    def _(offset):
        pl.semaphore_signal(barrier, inc=1, device_id=((me + offset) % shards, owner), device_id_type=MESH)

    pl.semaphore_signal(barrier, inc=1, device_id=(me, 1 - owner), device_id_type=MESH)
    pl.semaphore_wait(barrier, shards)

    def row_copy(way, slot, half, target, own=False):
        return pltpu.make_async_remote_copy(
            src_ref=packed.at[half] if own else rows_all.at[slot, half],
            dst_ref=rows_all.at[slot, half],
            send_sem=row_send.at[way, slot, half],
            recv_sem=row_recv.at[slot, half],
            device_id=(target, owner),
            device_id_type=MESH,
        )

    def arrived(slot, half):
        row_copy(ACROSS_X, slot, half, me + x_step).wait_recv()

    def along_z(way, slot, act, own=False):
        step = PLANE if way == UP else -PLANE

        @pl.when(z < LAYERS - 1 if way == UP else z > 0)
        def _():
            for half in range(2):
                act(row_copy(way, slot, half, me + step, own))

    def in_plane(slot, act, own=False):
        act(row_copy(ACROSS_X, slot, 0, me + x_step, own))
        act(row_copy(ACROSS_Y, slot, 1, me + y_step, own))
        act(row_copy(ACROSS_Y, slot, 0, me + y_step, own))
        act(row_copy(ACROSS_X, slot, 1, me + x_step, own))

    def relay(slot_x, slot_y, act, wait):
        if wait:
            arrived(slot_x, 0)
        act(row_copy(ACROSS_Y, slot_x, 0, me + y_step))
        if wait:
            arrived(slot_y, 1)
        act(row_copy(ACROSS_X, slot_y, 1, me + x_step))

    def layers_at(step, visit):
        if step == 0:
            visit(me, None)
            return

        @pl.when(z >= step)
        def _():
            visit(me - PLANE * step, UP)

        @pl.when(z + step < LAYERS)
        def _():
            visit(me + PLANE * step, DOWN)

    def gather_rows(act, wait):
        def first(slot, way):
            if way is None:
                along_z(UP, slot, act, True)
                along_z(DOWN, slot, act, True)
                in_plane(slot, act, True)
                return
            if wait:
                arrived(slot, 0)
                arrived(slot, 1)
            along_z(way, slot, act)
            in_plane(slot, act)

        def second(slot, way):
            relay(slot + x_step, slot + y_step, act, wait)

        layers_at(0, first)
        for step in range(1, LAYERS):
            layers_at(step, first)
            layers_at(step - 1, second)
        layers_at(LAYERS - 1, second)

    def diag_copy(offset, sender, target):
        return pltpu.make_async_remote_copy(
            src_ref=diagonal, dst_ref=diag_all.at[sender],
            send_sem=diag_send.at[offset], recv_sem=diag_recv.at[sender],
            device_id=(target, owner), device_id_type=MESH,
        )

    def term_copy(offset, sender, target):
        return pltpu.make_async_remote_copy(
            src_ref=terms.at[target // per], dst_ref=terms_all.at[sender],
            send_sem=term_send.at[offset], recv_sem=term_recv.at[sender],
            device_id=(target, owner), device_id_type=MESH,
        )

    def pair_copy(which, source, target):
        return pltpu.make_async_remote_copy(
            src_ref=source, dst_ref=target,
            send_sem=pair_send.at[which], recv_sem=pair_recv.at[which],
            device_id=(me, 1 - owner), device_id_type=MESH,
        )

    def to_all(make):
        @pl.loop(1, shards)
        def _(offset):
            make(offset, me, (me + offset) % shards).start()

    def wait_all(make):
        @pl.loop(1, shards)
        def _(offset):
            other = (me + offset) % shards
            make(offset, other, other).wait_recv()
            make(offset, me, other).wait_send()

    to_all(diag_copy)
    rows_all[me] = packed[...]
    diag_all[me] = diagonal[...]

    @pl.when(owner > 0)
    def _():
        pl.semaphore_wait(turn, 1)

    gather_rows(lambda copy: copy.start(), True)

    @pl.when(owner == 0)
    def _():
        pl.semaphore_signal(turn, inc=1, device_id=(me, 1 - owner), device_id_type=MESH)

    wait_all(diag_copy)
    for block in range(width // LANES):
        total = diag_all[block * per].astype(jnp.float32)
        for other in range(1, per):
            total += diag_all[block * per + other].astype(jnp.float32)
        diag_rows[:, block * LANES:(block + 1) * LANES] = total

    handover = pair_copy(0, outgoing, incoming)

    @pl.when(owner == 0)
    def _():
        incoming[...] = inflow[...]

    @pl.when(owner > 0)
    def _():
        handover.wait_recv()

    contract = (((1,), (1,)), ((), ()))

    def product(vector, layer, half, keep, others):
        group = rows_all.at[layer * PLANE:(layer + 1) * PLANE, half]
        middle = slice(layer * tile, (layer + 1) * tile)
        square = jnp.where(keep, group[:, :, middle].reshape(tile, tile), jnp.zeros((), jnp.bfloat16))
        total = lax.dot_general(
            vector[:, :, middle].reshape(2 * sources, tile), square, contract,
            preferred_element_type=jnp.float32,
        )
        if others.start < others.stop:
            count = others.stop - others.start
            total += lax.dot_general(
                vector[:, :, others].reshape(2 * sources, count),
                group[:, :, others].reshape(tile, count), contract,
                preferred_element_type=jnp.float32,
            )
        return total

    def complex_product(vector, layer, keep, others):
        real = product(vector, layer, 0, keep, others)
        imag = product(vector, layer, 1, keep, others)
        return real[:sources] - imag[sources:], imag[:sources] + real[sources:]

    row = lax.broadcasted_iota(jnp.int32, (tile, tile), 0)
    column = lax.broadcasted_iota(jnp.int32, (tile, tile), 1)

    for layer in range(LAYERS):
        slot = me % PLANE + layer * PLANE
        arrived(slot + x_step, 1)
        arrived(slot + y_step, 0)
        arrived(slot + x_step + y_step, 0)
        arrived(slot + x_step + y_step, 1)
        at = slice(layer * tile, (layer + 1) * tile)
        parts = complex_product(incoming, layer, column >= row, slice((layer + 1) * tile, width))
        ids = lax.broadcasted_iota(jnp.int32, (sources, tile), 1) + (owner * width + layer * tile)
        hit = ids == cell[...]
        for part in range(2):
            term = jnp.where(hit, wave[part], 0.0)
            reduced[part, :, at] = (term - parts[part]).astype(jnp.bfloat16)

    for layer in range(LAYERS):
        at = slice(layer * tile, (layer + 1) * tile)
        real, imag = complex_product(reduced, layer, column < row, slice(0, layer * tile))
        red_real, red_imag = (reduced[part, :, at].astype(jnp.float32) for part in range(2))
        diag_real, diag_imag = diag_rows[0:1, at], diag_rows[1:2, at]
        real = real + (red_real * diag_real - red_imag * diag_imag)
        imag = imag + (red_real * diag_imag + red_imag * diag_real)
        field[0, :, at] = real
        field[1, :, at] = imag
        outgoing[0, :, at] = real.astype(jnp.bfloat16)
        outgoing[1, :, at] = imag.astype(jnp.bfloat16)
        total = real * adjoint[0, :, at].astype(jnp.float32) + imag * adjoint[1, :, at].astype(jnp.float32)
        total = jnp.sum(total.reshape(sources // 8, 8, tile), axis=0) * scale
        for block in range(tile // LANES):
            terms[layer * (tile // LANES) + block] = total[:, block * LANES:(block + 1) * LANES]

    @pl.when(owner == 0)
    def _():
        handover.start()

    to_all(term_copy)
    local = receivers[...] - owner * width
    lane = local & (LANES - 1)
    home = local >> (LANES.bit_length() - 1)
    for part in range(2):
        values = jnp.zeros((sources, LANES), jnp.float32)
        for block in range(width // LANES):
            piece = field[part, :, block * LANES:(block + 1) * LANES]
            taken = jnp.take_along_axis(piece, lane, axis=1, mode="promise_in_bounds")
            values = jnp.where(home == block, taken, values)
        picked[part] = values.astype(jnp.bfloat16)
    swap = pair_copy(1, picked, picked_other)
    swap.start()

    wait_all(term_copy)
    total = terms[me // per]
    for offset in range(1, shards):
        total += terms_all[(me + offset) % shards]
    slab[...] = total

    gather_rows(lambda copy: copy.wait_send(), False)

    @pl.when(owner == 0)
    def _():
        handover.wait_send()

    swap.wait()
    both = picked[...].astype(jnp.float32) + picked_other[...].astype(jnp.float32)
    residual[...] = both - observed[...]


def per_device(
    lower_inverse,
    coupling,
    source_cell,
    source_wave,
    inflow_field,
    receiver_cell,
    observed,
    adjoint,
):
    me = lax.axis_index("src")
    shards = lax.axis_size("src")
    _, rows, _, width = lower_inverse.shape
    sources, receivers = receiver_cell.shape
    row_ids = me * rows + lax.broadcasted_iota(jnp.int32, (rows, width), 0)
    col_ids = lax.broadcasted_iota(jnp.int32, (rows, width), 1)
    lower = jnp.transpose(lower_inverse[0], (1, 0, 2))
    packed = jnp.where(col_ids < row_ids, lower, jnp.transpose(coupling[0], (1, 0, 2)))
    square = lax.dynamic_slice_in_dim(lower_inverse[0], me * rows, rows, axis=2)
    line = jnp.arange(rows)
    own = jnp.where((line[:, None] == line[None, :])[:, None, :], square, jnp.zeros((), square.dtype))
    own = jnp.sum(own.astype(jnp.float32), axis=0).astype(jnp.bfloat16)
    per = LANES // rows
    diagonal = lax.dynamic_update_slice(
        jnp.zeros((16, LANES), jnp.bfloat16), own, (jnp.int32(0), (me % per) * rows)
    )
    both = (2, sources, width)
    dma = pltpu.SemaphoreType.DMA
    vmem = pl.BlockSpec(memory_space=pltpu.VMEM)
    scale = 1.0 / math.sqrt(sources * shards)
    field, residual, slab = pl.pallas_call(
        functools.partial(window_kernel, scale),
        out_shape=(
            jax.ShapeDtypeStruct(both, jnp.float32),
            jax.ShapeDtypeStruct((2, sources, receivers), jnp.float32),
            jax.ShapeDtypeStruct((8, LANES), jnp.float32),
        ),
        in_specs=[vmem] * 8,
        out_specs=(vmem,) * 3,
        scratch_shapes=[
            pltpu.VMEM((shards, 2, rows, width), jnp.bfloat16),
            pltpu.VMEM((shards, 16, LANES), jnp.bfloat16),
            pltpu.VMEM((16, width), jnp.float32),
            pltpu.VMEM(both, jnp.bfloat16),
            pltpu.VMEM(both, jnp.bfloat16),
            pltpu.VMEM(both, jnp.bfloat16),
            pltpu.VMEM((width // LANES, 8, LANES), jnp.float32),
            pltpu.VMEM((shards, 8, LANES), jnp.float32),
            pltpu.VMEM((2, sources, LANES), jnp.bfloat16),
            pltpu.VMEM((2, sources, LANES), jnp.bfloat16),
            dma((4, shards, 2)),
            dma((shards, 2)),
            dma((shards,)),
            dma((shards,)),
            dma((shards,)),
            dma((shards,)),
            dma((2,)),
            dma((2,)),
            pltpu.SemaphoreType.REGULAR,
        ],
        compiler_params=pltpu.CompilerParams(
            collective_id=0, has_side_effects=True, vmem_limit_bytes=48 * 1024 * 1024
        ),
    )(
        packed,
        diagonal,
        jnp.transpose(inflow_field, (1, 0, 2)),
        source_cell[:, None],
        jnp.transpose(source_wave)[:, :, None],
        receiver_cell,
        jnp.transpose(observed, (1, 0, 2)),
        jnp.transpose(adjoint[:, 0], (1, 0, 2)),
    )
    gradient = lax.dynamic_slice_in_dim(jnp.sum(slab, axis=0), (me % per) * rows, rows)
    return (
        jnp.transpose(field, (1, 0, 2))[:, None],
        jnp.transpose(residual, (1, 0, 2)),
        gradient[None],
    )


def solution(mesh):
    fits = mesh.shape["src"] == PLANE * LAYERS and mesh.shape["fac"] == 2
    placed = (
        P("fac", "src", None, None),
        P("fac", "src", None, None),
        P("src"),
        P("src", None),
        P("src", None, None),
        P("src", None),
        P("src", None, None),
        P("src", "fac", None, None),
    )
    return jax.shard_map(
        per_device if fits else plain_device,
        mesh=mesh,
        in_specs=placed,
        out_specs=(P("src", "fac", None, None), P("src", None, None), P("fac", "src")),
        check_vma=False,
    )
```

```python
import functools
import math

import jax
import jax.numpy as jnp
from jax import lax
from jax.experimental import pallas as pl
from jax.experimental.pallas import tpu as pltpu
from jax.sharding import PartitionSpec as P

MESH = pl.DeviceIdType.MESH
LANES = 128
UP, DOWN, ACROSS_X, ACROSS_Y = range(4)
PLANE, LAYERS = 4, 4


def from_behind(shard, axis, by):
    size = lax.axis_size(axis)
    pairs = [(i, i + by) for i in range(size) if 0 <= i + by < size]
    return lax.ppermute(shard, axis, pairs)


def complex_apply(vector, matrix):
    width = matrix.shape[0]
    joined = matrix.reshape(width, 2 * width)
    real_row = jnp.concatenate([vector[:, 0], -vector[:, 1]], axis=1)
    imag_row = jnp.concatenate([vector[:, 1], vector[:, 0]], axis=1)
    stacked = jnp.stack([real_row, imag_row], axis=1).reshape(-1, 2 * width)
    contract_dims = (((1,), (1,)), ((), ()))
    result = lax.dot_general(stacked, joined, contract_dims, preferred_element_type=jnp.float32)
    return result.reshape(vector.shape[0], 2, width)


def source_block(cells, wave, owner, width):
    cell_ids = owner * width + lax.broadcasted_iota(jnp.int32, (width,), 0)
    hit = cells[:, None] == cell_ids[None, :]
    return jnp.where(hit[:, None, :], wave[:, :, None], jnp.zeros((), jnp.float32))


def block_solve(previous, cells, wave, owner, lower_full, coupling_full):
    width = lower_full.shape[0]
    term = source_block(cells, wave, owner, width)
    reduced = (term - complex_apply(previous, coupling_full)).astype(jnp.bfloat16)
    return complex_apply(reduced, lower_full)


def plain_device(
    lower_inverse,
    coupling,
    source_cell,
    source_wave,
    inflow_field,
    receiver_cell,
    observed,
    adjoint,
):
    owner = lax.axis_index("fac")
    fac_count = lax.axis_size("fac")
    width = lower_inverse.shape[3]
    sources = source_cell.shape[0]
    whole_lower, whole_coupling = (
        lax.all_gather(lower_inverse, "src", axis=1, tiled=True),
        lax.all_gather(coupling, "src", axis=1, tiled=True),
    )
    lower_full = whole_lower[0]
    coupling_full = whole_coupling[0]
    empty_field = jnp.zeros((sources, 2, width), jnp.float32)

    def section_step(section, carry):
        current, received = carry

        def compute():
            return block_solve(received, source_cell, source_wave, owner, lower_full, coupling_full)

        def unchanged():
            return current

        current = lax.cond(section == owner, compute, unchanged)
        received = from_behind(current.astype(jnp.bfloat16), "fac", 1)
        return (current, received)

    current, received = lax.fori_loop(0, fac_count, section_step, (empty_field, inflow_field))
    local_ids = receiver_cell - owner * width
    inside = (local_ids >= 0) & (local_ids < width)
    clipped = jnp.clip(local_ids, 0, width - 1)
    index_both = jnp.broadcast_to(clipped[:, None, :], observed.shape)
    values = jnp.take_along_axis(current, index_both, axis=2)
    values = jnp.where(inside[:, None, :], values, jnp.zeros((), jnp.float32))
    picked = lax.psum(values.astype(jnp.bfloat16), "fac").astype(jnp.float32)
    scale = 1.0 / math.sqrt(sources * lax.axis_size("src"))
    terms = jnp.sum(current * adjoint[:, 0].astype(jnp.float32), axis=(0, 1)) * scale
    gradient = lax.psum_scatter(terms[None, :], "src", scatter_dimension=1, tiled=True)
    return (current[:, None], picked - observed, gradient)


def window_kernel(
    scale, packed, diagonal, inflow, cell, wave, receivers_far, adjoint,
    field, residual, slab,
    rows_all, diag_all, diag_rows, incoming, reduced, outgoing, terms, terms_all, picked, picked_other,
    row_send, row_recv, diag_send, diag_recv, term_send, term_recv, pair_send, pair_recv, turn, receivers, receivers_done,
):
    me, owner = lax.axis_index("src"), lax.axis_index("fac")
    shards = PLANE * LAYERS
    x, y, z = me % 2, (me // 2) % 2, me // PLANE
    x_step, y_step = 1 - 2 * x, 2 - 4 * y
    _, sources, width = field.shape
    rows = packed.shape[1]
    per = LANES // rows
    tile = PLANE * rows

    barrier = pltpu.get_barrier_semaphore()

    @pl.loop(1, shards)
    def _(offset):
        pl.semaphore_signal(barrier, inc=1, device_id=((me + offset) % shards, owner), device_id_type=MESH)

    pl.semaphore_signal(barrier, inc=1, device_id=(me, 1 - owner), device_id_type=MESH)
    pl.semaphore_wait(barrier, shards)

    def row_copy(way, slot, half, target, own=False):
        return pltpu.make_async_remote_copy(
            src_ref=packed.at[half] if own else rows_all.at[slot, half],
            dst_ref=rows_all.at[slot, half],
            send_sem=row_send.at[way, slot, half],
            recv_sem=row_recv.at[slot, half],
            device_id=(target, owner),
            device_id_type=MESH,
        )

    def arrived(slot, half):
        row_copy(ACROSS_X, slot, half, me + x_step).wait_recv()

    def along_z(way, slot, act, own=False):
        step = PLANE if way == UP else -PLANE

        @pl.when(z < LAYERS - 1 if way == UP else z > 0)
        def _():
            for half in range(2):
                act(row_copy(way, slot, half, me + step, own))

    def in_plane(slot, act, own=False):
        act(row_copy(ACROSS_X, slot, 0, me + x_step, own))
        act(row_copy(ACROSS_Y, slot, 1, me + y_step, own))
        act(row_copy(ACROSS_Y, slot, 0, me + y_step, own))
        act(row_copy(ACROSS_X, slot, 1, me + x_step, own))

    def relay(slot_x, slot_y, act, wait):
        if wait:
            arrived(slot_x, 0)
        act(row_copy(ACROSS_Y, slot_x, 0, me + y_step))
        if wait:
            arrived(slot_y, 1)
        act(row_copy(ACROSS_X, slot_y, 1, me + x_step))

    def layers_at(step, visit):
        if step == 0:
            visit(me, None)
            return

        @pl.when(z >= step)
        def _():
            visit(me - PLANE * step, UP)

        @pl.when(z + step < LAYERS)
        def _():
            visit(me + PLANE * step, DOWN)

    def gather_rows(act, wait, midway=None):
        def first(slot, way):
            if way is None:
                along_z(UP, slot, act, True)
                along_z(DOWN, slot, act, True)
                in_plane(slot, act, True)
                return
            if wait:
                arrived(slot, 0)
                arrived(slot, 1)
            along_z(way, slot, act)
            in_plane(slot, act)

        def second(slot, way):
            relay(slot + x_step, slot + y_step, act, wait)

        layers_at(0, first)
        for step in range(1, LAYERS):
            layers_at(step, first)
            if midway is not None and step == 2:
                midway()
            layers_at(step - 1, second)
        layers_at(LAYERS - 1, second)

    def diag_copy(offset, sender, target):
        return pltpu.make_async_remote_copy(
            src_ref=diagonal, dst_ref=diag_all.at[sender],
            send_sem=diag_send.at[offset], recv_sem=diag_recv.at[sender],
            device_id=(target, owner), device_id_type=MESH,
        )

    def term_copy(offset, sender, target):
        return pltpu.make_async_remote_copy(
            src_ref=terms.at[target // per], dst_ref=terms_all.at[sender],
            send_sem=term_send.at[offset], recv_sem=term_recv.at[sender],
            device_id=(target, owner), device_id_type=MESH,
        )

    def pair_copy(which, source, target):
        return pltpu.make_async_remote_copy(
            src_ref=source, dst_ref=target,
            send_sem=pair_send.at[which], recv_sem=pair_recv.at[which],
            device_id=(me, 1 - owner), device_id_type=MESH,
        )

    def to_all(make):
        @pl.loop(1, shards)
        def _(offset):
            make(offset, me, (me + offset) % shards).start()

    def wait_all(make):
        @pl.loop(1, shards)
        def _(offset):
            other = (me + offset) % shards
            make(offset, other, other).wait_recv()
            make(offset, me, other).wait_send()

    receivers_copy = pltpu.make_async_copy(receivers_far, receivers, receivers_done)
    receivers_copy.start()
    to_all(diag_copy)
    rows_all[me] = packed[...]
    diag_all[me] = diagonal[...]

    @pl.when(owner > 0)
    def _():
        pl.semaphore_wait(turn, 1)

    def pass_turn():
        @pl.when(owner == 0)
        def _():
            pl.semaphore_signal(turn, inc=1, device_id=(me, 1 - owner), device_id_type=MESH)

    gather_rows(lambda copy: copy.start(), True, pass_turn)
    wait_all(diag_copy)
    for block in range(width // LANES):
        total = diag_all[block * per].astype(jnp.float32)
        for other in range(1, per):
            total += diag_all[block * per + other].astype(jnp.float32)
        diag_rows[:, block * LANES:(block + 1) * LANES] = total

    handover = pair_copy(0, outgoing, incoming)

    @pl.when(owner == 0)
    def _():
        incoming[...] = inflow[...]

    @pl.when(owner > 0)
    def _():
        handover.wait_recv()

    contract = (((1,), (1,)), ((), ()))

    def product(vector, layer, half, keep, others):
        group = rows_all.at[layer * PLANE:(layer + 1) * PLANE, half]
        middle = slice(layer * tile, (layer + 1) * tile)
        square = jnp.where(keep, group[:, :, middle].reshape(tile, tile), jnp.zeros((), jnp.bfloat16))
        total = lax.dot_general(
            vector[:, :, middle].reshape(2 * sources, tile), square, contract,
            preferred_element_type=jnp.float32,
        )
        if others.start < others.stop:
            count = others.stop - others.start
            total += lax.dot_general(
                vector[:, :, others].reshape(2 * sources, count),
                group[:, :, others].reshape(tile, count), contract,
                preferred_element_type=jnp.float32,
            )
        return total

    def complex_product(vector, layer, keep, others):
        real = product(vector, layer, 0, keep, others)
        imag = product(vector, layer, 1, keep, others)
        return real[:sources] - imag[sources:], imag[:sources] + real[sources:]

    row = lax.broadcasted_iota(jnp.int32, (tile, tile), 0)
    column = lax.broadcasted_iota(jnp.int32, (tile, tile), 1)

    def reduce_layer(layer):
        slot = me % PLANE + layer * PLANE
        arrived(slot + x_step, 1)
        arrived(slot + y_step, 0)
        arrived(slot + x_step + y_step, 0)
        arrived(slot + x_step + y_step, 1)
        at = slice(layer * tile, (layer + 1) * tile)
        parts = complex_product(incoming, layer, column >= row, slice((layer + 1) * tile, width))
        ids = lax.broadcasted_iota(jnp.int32, (sources, tile), 1) + (owner * width + layer * tile)
        hit = ids == cell[...]
        for part in range(2):
            term = jnp.where(hit, wave[part], 0.0)
            reduced[part, :, at] = (term - parts[part]).astype(jnp.bfloat16)

    @pl.when(z < LAYERS // 2)
    def _():
        for layer in range(LAYERS):
            reduce_layer(layer)

    @pl.when(z >= LAYERS // 2)
    def _():
        for layer in reversed(range(LAYERS)):
            reduce_layer(layer)

    for layer in range(LAYERS):
        at = slice(layer * tile, (layer + 1) * tile)
        real, imag = complex_product(reduced, layer, column < row, slice(0, layer * tile))
        red_real, red_imag = (reduced[part, :, at].astype(jnp.float32) for part in range(2))
        diag_real, diag_imag = diag_rows[0:1, at], diag_rows[1:2, at]
        real = real + (red_real * diag_real - red_imag * diag_imag)
        imag = imag + (red_real * diag_imag + red_imag * diag_real)
        field[0, :, at] = real
        field[1, :, at] = imag
        outgoing[0, :, at] = real.astype(jnp.bfloat16)
        outgoing[1, :, at] = imag.astype(jnp.bfloat16)
        total = real * adjoint[0, :, at].astype(jnp.float32) + imag * adjoint[1, :, at].astype(jnp.float32)
        total = jnp.sum(total.reshape(sources // 8, 8, tile), axis=0) * scale
        for block in range(tile // LANES):
            terms[layer * (tile // LANES) + block] = total[:, block * LANES:(block + 1) * LANES]
        for target in range(layer * PLANE, (layer + 1) * PLANE):

            @pl.when(me != target)
            def _(target=target):
                term_copy(target, me, target).start()

    @pl.when(owner == 0)
    def _():
        handover.start()

    receivers_copy.wait()
    local = receivers[...] - owner * width
    lane = local & (LANES - 1)
    home = local >> (LANES.bit_length() - 1)
    for part in range(2):
        values = jnp.zeros((sources, LANES), jnp.float32)
        for block in range(width // LANES):
            piece = field[part, :, block * LANES:(block + 1) * LANES]
            taken = jnp.take_along_axis(piece, lane, axis=1, mode="promise_in_bounds")
            values = jnp.where(home == block, taken, values)
        picked[part] = values.astype(jnp.bfloat16)
    swap = pair_copy(1, picked, picked_other)
    swap.start()

    @pl.loop(1, shards)
    def _(offset):
        other = (me + offset) % shards
        term_copy(other, other, other).wait_recv()
        term_copy(other, me, other).wait_send()

    total = terms[me // per]
    for offset in range(1, shards):
        total += terms_all[(me + offset) % shards]
    slab[...] = total

    gather_rows(lambda copy: copy.wait_send(), False)

    @pl.when(owner == 0)
    def _():
        handover.wait_send()

    swap.wait()
    both = picked[...].astype(jnp.float32) + picked_other[...].astype(jnp.float32)
    residual[...] = both


def per_device(
    lower_inverse,
    coupling,
    source_cell,
    source_wave,
    inflow_field,
    receiver_cell,
    observed,
    adjoint,
):
    me = lax.axis_index("src")
    shards = lax.axis_size("src")
    _, rows, _, width = lower_inverse.shape
    sources, receivers = receiver_cell.shape
    row_ids = me * rows + lax.broadcasted_iota(jnp.int32, (rows, width), 0)
    col_ids = lax.broadcasted_iota(jnp.int32, (rows, width), 1)
    lower = jnp.transpose(lower_inverse[0], (1, 0, 2))
    packed = jnp.where(col_ids < row_ids, lower, jnp.transpose(coupling[0], (1, 0, 2)))
    square = lax.dynamic_slice_in_dim(lower_inverse[0], me * rows, rows, axis=2)
    line = jnp.arange(rows)
    own = jnp.where((line[:, None] == line[None, :])[:, None, :], square, jnp.zeros((), square.dtype))
    own = jnp.sum(own.astype(jnp.float32), axis=0).astype(jnp.bfloat16)
    per = LANES // rows
    diagonal = lax.dynamic_update_slice(
        jnp.zeros((16, LANES), jnp.bfloat16), own, (jnp.int32(0), (me % per) * rows)
    )
    both = (2, sources, width)
    dma = pltpu.SemaphoreType.DMA
    vmem = pl.BlockSpec(memory_space=pltpu.VMEM)
    scale = 1.0 / math.sqrt(sources * shards)
    field, residual, slab = pl.pallas_call(
        functools.partial(window_kernel, scale),
        out_shape=(
            jax.ShapeDtypeStruct(both, jnp.float32),
            jax.ShapeDtypeStruct((2, sources, receivers), jnp.float32),
            jax.ShapeDtypeStruct((8, LANES), jnp.float32),
        ),
        in_specs=[vmem] * 5 + [pl.BlockSpec(memory_space=pl.ANY), vmem],
        out_specs=(vmem,) * 3,
        scratch_shapes=[
            pltpu.VMEM((shards, 2, rows, width), jnp.bfloat16),
            pltpu.VMEM((shards, 16, LANES), jnp.bfloat16),
            pltpu.VMEM((16, width), jnp.float32),
            pltpu.VMEM(both, jnp.bfloat16),
            pltpu.VMEM(both, jnp.bfloat16),
            pltpu.VMEM(both, jnp.bfloat16),
            pltpu.VMEM((width // LANES, 8, LANES), jnp.float32),
            pltpu.VMEM((shards, 8, LANES), jnp.float32),
            pltpu.VMEM((2, sources, LANES), jnp.bfloat16),
            pltpu.VMEM((2, sources, LANES), jnp.bfloat16),
            dma((4, shards, 2)),
            dma((shards, 2)),
            dma((shards,)),
            dma((shards,)),
            dma((shards,)),
            dma((shards,)),
            dma((2,)),
            dma((2,)),
            pltpu.SemaphoreType.REGULAR,
            pltpu.VMEM((sources, receivers), jnp.int32),
            dma,
        ],
        compiler_params=pltpu.CompilerParams(
            collective_id=0, has_side_effects=True, vmem_limit_bytes=48 * 1024 * 1024
        ),
    )(
        packed,
        diagonal,
        jnp.transpose(inflow_field, (1, 0, 2)),
        source_cell[:, None],
        jnp.transpose(source_wave)[:, :, None],
        receiver_cell,
        jnp.transpose(adjoint[:, 0], (1, 0, 2)),
    )
    gradient = lax.dynamic_slice_in_dim(jnp.sum(slab, axis=0), (me % per) * rows, rows)
    return (
        jnp.transpose(field, (1, 0, 2))[:, None],
        jnp.transpose(residual, (1, 0, 2)) - observed,
        gradient[None],
    )


def solution(mesh):
    fits = mesh.shape["src"] == PLANE * LAYERS and mesh.shape["fac"] == 2
    placed = (
        P("fac", "src", None, None),
        P("fac", "src", None, None),
        P("src"),
        P("src", None),
        P("src", None, None),
        P("src", None),
        P("src", None, None),
        P("src", "fac", None, None),
    )
    return jax.shard_map(
        per_device if fits else plain_device,
        mesh=mesh,
        in_specs=placed,
        out_specs=(P("src", "fac", None, None), P("src", None, None), P("fac", "src")),
        check_vma=False,
    )
```
